32 devices in a mesh: outer: 2 (over x), inner: 16 (over z, y, core).
Axes of the slice: x: 2, y: 2, z: 4, core: 2. Of those that a mesh axis runs over, the one named last changes fastest.
Arguments:
- query_stream: float32 [16384, 128], P(('outer', 'inner')), may hold values from -6 to 6
- key_stream: float32 [16384, 128], P(('outer', 'inner')), may hold values from -6 to 6
- value_stream: float32 [16384, 128], P(('outer', 'inner')), may hold values from -6 to 6
- filter_taps: float32 [16384, 128], P(('outer', 'inner')), may hold values from -1.6 to 1.6
- skip_gain: float32 [128], replicated, may hold values from -1 to 1
- short_weights: float32 [3, 3, 128], replicated, may hold values from -3 to 3
- cotangent: float32 [16384, 128], P(('outer', 'inner')), may hold values from -10 to 10
Outputs:
- gated_output: float32 [16384, 128], P(('outer', 'inner'))
- stream_grads: float32 [3, 16384, 128], P(None, ('outer', 'inner'))
- filter_grad: float32 [16384, 128], P(('outer', 'inner'))
- tap_grads: float32 [3, 3, 128], replicated
- skip_grad: float32 [128], replicated
The draws below stay inside these ranges and needn't reach their ends.
All inputs are finite; a program needn't handle non-finite values.
Results may differ from the reference program's by a relative error of at most 0.0003.
Values sent between devices are 32-bit elements; how exact they have to be, the bound alone decides.
A program may use at most 64 MiB of HBM per device.

```python
import math
import jax
import jax.numpy as jnp
from jax import lax

CH = 128
SEQ = 16384


def draw_filter_taps(key, part):
    folded = jax.random.fold_in(key, 11)
    rate_key, jitter_key = jax.random.split(folded)
    positions = jnp.arange(SEQ, dtype=jnp.float32)[:, None]
    lifetime = jnp.exp(jax.random.uniform(rate_key, (1, CH), jnp.float32, math.log(30.0), math.log(4.0 * SEQ)))
    jitter = jax.random.truncated_normal(jitter_key, -6.0, 6.0, (SEQ, CH), jnp.float32)
    amplitude = jnp.sqrt(2.0 / jnp.minimum(lifetime, float(SEQ)))
    return (jitter * amplitude * jnp.exp(-positions / lifetime)).astype(jnp.float32)


def draw_cotangent(key, part):
    folded = jax.random.fold_in(key, 23)
    positions = jnp.arange(SEQ, dtype=jnp.float32)[:, None] / float(SEQ)
    envelope = 0.5 + 1.5 * positions
    jitter = jax.random.truncated_normal(folded, -5.0, 5.0, (SEQ, CH), jnp.float32) * envelope
    return jitter.astype(jnp.float32)


def block_levels(stream_key, dims, shards, low, largest):
    def one(axis_at, blocks):
        steps = jax.random.uniform(jax.random.fold_in(jax.random.fold_in(stream_key, 6), axis_at), (blocks,), jnp.float32, low / len(shards), largest / len(shards))
        return jnp.repeat(jnp.exp(steps), dims[axis_at] // blocks).reshape((-1,) + (1,) * (len(dims) - axis_at - 1))

    factor_of = one(*shards[0])
    for cut in shards[1:]:
        factor_of = factor_of * one(*cut)
    return factor_of


def bell_draw(key, dims, spread, bound, cuts=(), kind=jnp.bfloat16):
    entries = spread * jax.random.normal(key, dims, jnp.float32)
    if cuts:
        entries = entries * block_levels(key, dims, cuts, -0.22, 0.18)
    return jnp.clip(entries, -bound, bound).astype(kind)


def setup_inputs(seed: int = 0) -> dict:
    key_of = jax.random.split(jax.random.key(seed), 8)
    return {
        "query_stream": bell_draw(key_of[0], (SEQ, CH), 1.0, 6.0, ((0, 32),), jnp.float32),
        "key_stream": bell_draw(key_of[1], (SEQ, CH), 1.0, 6.0, ((0, 32),), jnp.float32),
        "value_stream": bell_draw(key_of[2], (SEQ, CH), 1.0, 6.0, ((0, 32),), jnp.float32),
        "filter_taps": draw_filter_taps(jax.random.fold_in(key_of[7], 71), 0),
        "skip_gain": jnp.clip(jax.random.uniform(key_of[4], (CH,), jnp.float32, -1.0, 1.0), -1.0, 1.0),
        "short_weights": bell_draw(key_of[5], (3, 3, CH), 0.6, 3.0, (), jnp.float32),
        "cotangent": draw_cotangent(jax.random.fold_in(key_of[7], 71), 0),
    }


def causal_taps(streams, weights):
    padded = jnp.pad(streams, ((0, 0), (2, 0), (0, 0)))
    lag_one = padded[:, 1:-1]
    lag_two = padded[:, :-2]
    mixed = weights[:, 0:1] * streams + weights[:, 1:2] * lag_one + weights[:, 2:3] * lag_two
    return (mixed, lag_one, lag_two)

def long_terms(block):
    extent = block.shape[1]
    length = 2 * extent
    spectra = jnp.fft.rfft(block, n=length, axis=1)
    filter_spec = spectra[0]
    product_spec = spectra[1]
    upstream_spec = spectra[2]
    causal = jnp.fft.irfft(filter_spec * product_spec, n=length, axis=0)[:extent]
    backward = jnp.fft.irfft(jnp.conj(filter_spec) * upstream_spec, n=length, axis=0)[:extent]
    gradient = jnp.fft.irfft(jnp.conj(product_spec) * upstream_spec, n=length, axis=0)[:extent]
    return jnp.stack([causal, backward, gradient])

def reference(query_stream, key_stream, value_stream, filter_taps, skip_gain, short_weights, cotangent):
    streams = jnp.stack([query_stream, key_stream, value_stream])
    mixed, lag_one, lag_two = causal_taps(streams, short_weights)
    product = mixed[1] * mixed[2]
    upstream = cotangent * mixed[0]
    stacked = jnp.stack([filter_taps, product, upstream])
    blocks = CH // 16
    shaped = stacked.reshape(3, SEQ, blocks, 16).transpose(2, 0, 1, 3)
    longs = lax.map(long_terms, shaped).transpose(1, 2, 0, 3).reshape(3, SEQ, CH)
    summed = longs[0] + skip_gain * product
    gated_output = mixed[0] * summed
    backward = longs[1] + skip_gain * upstream
    grads = jnp.stack([cotangent * summed, backward * mixed[2], backward * mixed[1]])
    padded = jnp.pad(grads, ((0, 0), (0, 2), (0, 0)))
    stream_grads = short_weights[:, 0:1] * grads + short_weights[:, 1:2] * padded[:, 1:-1] + short_weights[:, 2:3] * padded[:, 2:]
    factor = 1.0 / math.sqrt(SEQ)
    tap_grads = jnp.stack([lax.optimization_barrier(jnp.sum(grads * streams, axis=1)), lax.optimization_barrier(jnp.sum(grads * lag_one, axis=1)), lax.optimization_barrier(jnp.sum(grads * lag_two, axis=1))], axis=1) * factor
    skip_grad = lax.optimization_barrier(jnp.sum(upstream * product, axis=0)) * factor
    filter_grad = longs[2] * factor
    return (gated_output, stream_grads, filter_grad, tap_grads, skip_grad)
```

```python
import functools
import math

import jax
import jax.numpy as jnp
import ml_dtypes
import numpy as np
from jax import lax
from jax.experimental import pallas as pl
from jax.experimental.pallas import tpu as pltpu
from jax.sharding import PartitionSpec as P

MESH = pl.DeviceIdType.MESH

exact_mode = lax.Precision.HIGHEST


def passed_along(block, axis, distance):
    devices = range(lax.axis_size(axis))
    route = [(i - distance, i) for i in devices if i - distance in devices]
    return lax.ppermute(block, axis, route)


def unit_angles(counts_table, period):
    return 2.0 * math.pi / period * (counts_table % period).astype(jnp.float32)


def turned(real_part, imag_part, cosine, sine, sign):
    return (
        real_part * cosine - sign * imag_part * sine,
        imag_part * cosine + sign * real_part * sine,
    )


def applied(formula, angles, real_part, imag_part, sign):
    cosine = jnp.cos(angles)
    sine = jnp.sin(angles)
    cos_real = jnp.einsum(formula, cosine, real_part, precision=exact_mode)
    cos_imag = jnp.einsum(formula, cosine, imag_part, precision=exact_mode)
    sin_real = jnp.einsum(formula, sine, real_part, precision=exact_mode)
    sin_imag = jnp.einsum(formula, sine, imag_part, precision=exact_mode)
    return (cos_real - sign * sin_imag, cos_imag + sign * sin_real)


def sequence_blocks(tiles):
    groups, devices, tile_size = tiles.shape
    shaped = tiles.reshape(groups, lax.axis_size("outer"), lax.axis_size("inner"), 1, 1, tile_size)
    moved = lax.all_to_all(
        lax.all_to_all(shaped, "outer", split_axis=1, concat_axis=3, tiled=True),
        "inner",
        split_axis=2,
        concat_axis=4,
        tiled=True,
    )
    return moved.reshape(groups, devices, tile_size)


def spectral_blocks(tiles):
    groups, devices, tile_size = tiles.shape
    shaped = tiles.reshape(groups, lax.axis_size("outer"), lax.axis_size("inner"), 1, 1, tile_size)
    moved = lax.all_to_all(
        lax.all_to_all(shaped, "outer", split_axis=1, concat_axis=3, tiled=True),
        "inner",
        split_axis=2,
        concat_axis=4,
        tiled=True,
    )
    return moved.reshape(groups, devices, tile_size)


def self_position():
    return lax.axis_index("outer") * lax.axis_size("inner") + lax.axis_index("inner")


def local_forward(real_part, imag_part):
    members, pairs, row_count, channels = real_part.shape
    second = row_count // 16
    first_index = jnp.arange(16, dtype=jnp.int32)
    second_index = jnp.arange(second, dtype=jnp.int32)
    real_part = real_part.reshape(members, pairs, 16, second, channels)
    imag_part = imag_part.reshape(members, pairs, 16, second, channels)
    first_angles = unit_angles(first_index[:, None] * first_index[None, :], 16)
    real_part, imag_part = applied("ka,mtacx->mtkcx", first_angles, real_part, imag_part, -1.0)
    twiddle = unit_angles(first_index[:, None] * second_index[None, :], row_count)[:, :, None]
    real_part, imag_part = turned(real_part, imag_part, jnp.cos(twiddle), jnp.sin(twiddle), -1.0)
    second_angles = unit_angles(second_index[:, None] * second_index[None, :], second)
    real_part, imag_part = applied("qc,mtkcx->mtqkx", second_angles, real_part, imag_part, -1.0)
    return (
        real_part.reshape(members, pairs, row_count, channels),
        imag_part.reshape(members, pairs, row_count, channels),
    )


def local_inverse(real_part, imag_part):
    members, pairs, row_count, channels = real_part.shape
    second = row_count // 16
    first_index = jnp.arange(16, dtype=jnp.int32)
    second_index = jnp.arange(second, dtype=jnp.int32)
    real_part = real_part.reshape(members, pairs, second, 16, channels)
    imag_part = imag_part.reshape(members, pairs, second, 16, channels)
    second_angles = unit_angles(second_index[:, None] * second_index[None, :], second)
    real_part, imag_part = applied("cq,mtqkx->mtckx", second_angles, real_part, imag_part, 1.0)
    twiddle = unit_angles(second_index[:, None] * first_index[None, :], row_count)[:, :, None]
    real_part, imag_part = turned(real_part, imag_part, jnp.cos(twiddle), jnp.sin(twiddle), 1.0)
    first_angles = unit_angles(first_index[:, None] * first_index[None, :], 16)
    real_part, imag_part = applied("ak,mtckx->mtacx", first_angles, real_part, imag_part, 1.0)
    return (
        real_part.reshape(members, pairs, row_count, channels),
        imag_part.reshape(members, pairs, row_count, channels),
    )


def fourier_forward(signals):
    members, row_count, channels = signals.shape
    devices = lax.axis_size("outer") * lax.axis_size("inner")
    tile_rows = row_count // devices
    length = 2 * row_count * devices
    columns = sequence_blocks(signals.reshape(members, devices, tile_rows * channels))
    parity = jnp.arange(2, dtype=jnp.int32)
    target = jnp.arange(devices, dtype=jnp.int32)
    frequency = 2 * target[None, :] + parity[:, None]
    angles = unit_angles(frequency[:, :, None] * target[None, None, :], 2 * devices)
    first_real = jnp.einsum("tdb,mbx->mtdx", jnp.cos(angles), columns, precision=exact_mode)
    first_imag = -jnp.einsum("tdb,mbx->mtdx", jnp.sin(angles), columns, precision=exact_mode)
    first_real = first_real.reshape(members, 2, devices, tile_rows, channels)
    first_imag = first_imag.reshape(members, 2, devices, tile_rows, channels)
    offset = self_position() * tile_rows + jnp.arange(tile_rows, dtype=jnp.int32)
    twiddle = unit_angles(frequency[:, :, None] * offset[None, None, :], length)[:, :, :, None]
    first_real, first_imag = turned(
        first_real, first_imag, jnp.cos(twiddle), jnp.sin(twiddle), -1.0
    )
    stacked = jnp.stack([first_real, first_imag], axis=1).reshape(
        members * 4, devices, tile_rows * channels
    )
    spread = spectral_blocks(stacked).reshape(members, 2, 2, row_count, channels)
    return local_forward(spread[:, 0], spread[:, 1])


def fourier_inverse(real_part, imag_part):
    members, pairs, row_count, channels = real_part.shape
    devices = lax.axis_size("outer") * lax.axis_size("inner")
    tile_rows = row_count // devices
    length = 2 * row_count * devices
    real_part, imag_part = local_inverse(real_part, imag_part)
    parity = jnp.arange(2, dtype=jnp.int32)
    frequency = 2 * self_position() + parity
    twiddle = unit_angles(
        frequency[:, None] * jnp.arange(row_count, dtype=jnp.int32)[None, :], length
    )[:, :, None]
    real_part, imag_part = turned(real_part, imag_part, jnp.cos(twiddle), jnp.sin(twiddle), 1.0)
    stacked = jnp.stack([real_part, imag_part], axis=1).reshape(
        members * 4, devices, tile_rows * channels
    )
    gathered = spectral_blocks(stacked).reshape(members, 2, 2, devices, tile_rows * channels)
    target = jnp.arange(devices, dtype=jnp.int32)
    angles = unit_angles(
        target[:, None, None] * (2 * target[None, None, :] + parity[None, :, None]), 2 * devices
    )
    cosine = jnp.cos(angles)
    sine = jnp.sin(angles)
    scale = 1.0 / length
    real_out = (
        jnp.einsum("btd,mtdx->mbx", cosine, gathered[:, 0], precision=exact_mode)
        - jnp.einsum("btd,mtdx->mbx", sine, gathered[:, 1], precision=exact_mode)
    ) * scale
    imag_out = real_out[:0]
    return (real_out, imag_out)


def on_device(
    query_stream, key_stream, value_stream, filter_taps, skip_gain, short_weights, cotangent
):
    row_count, channels = query_stream.shape
    devices = lax.axis_size("outer") * lax.axis_size("inner")
    streams = jnp.stack([query_stream, key_stream, value_stream])
    earlier = passed_along(streams[:, row_count - 2 :, :], ("outer", "inner"), 1)
    ahead = jnp.concatenate([earlier, streams], axis=1)
    lag_one = ahead[:, 1 : row_count + 1]
    lag_two = ahead[:, 0:row_count]
    mixed = (
        short_weights[:, 0:1] * streams
        + short_weights[:, 1:2] * lag_one
        + short_weights[:, 2:3] * lag_two
    )
    product = mixed[1] * mixed[2]
    upstream = cotangent * mixed[0]
    spec_real, spec_imag = fourier_forward(jnp.stack([filter_taps, product, upstream]))
    filter_real, product_real, upstream_real = (spec_real[0], spec_real[1], spec_real[2])
    filter_imag, product_imag, upstream_imag = (spec_imag[0], spec_imag[1], spec_imag[2])
    causal_real = filter_real * product_real - filter_imag * product_imag
    causal_imag = filter_real * product_imag + filter_imag * product_real
    back_real = filter_real * upstream_real + filter_imag * upstream_imag
    back_imag = filter_real * upstream_imag - filter_imag * upstream_real
    grad_real = product_real * upstream_real + product_imag * upstream_imag
    grad_imag = product_real * upstream_imag - product_imag * upstream_real
    real_out, imag_out = fourier_inverse(
        jnp.stack([causal_real, back_real, grad_real]),
        jnp.stack([causal_imag, back_imag, grad_imag]),
    )
    longs = sequence_blocks(real_out).reshape(3, row_count, channels)
    summed = longs[0] + skip_gain * product
    gated_output = mixed[0] * summed
    backward = longs[1] + skip_gain * upstream
    grads = jnp.stack([cotangent * summed, backward * mixed[2], backward * mixed[1]])
    later = passed_along(grads[:, 0:2, :], ("outer", "inner"), -1)
    behind = jnp.concatenate([grads, later], axis=1)
    stream_grads = (
        short_weights[:, 0:1] * grads
        + short_weights[:, 1:2] * behind[:, 1 : row_count + 1]
        + short_weights[:, 2:3] * behind[:, 2 : row_count + 2]
    )
    tap_terms = jnp.stack(
        [
            jnp.sum(grads * streams, axis=1),
            jnp.sum(grads * lag_one, axis=1),
            jnp.sum(grads * lag_two, axis=1),
        ],
        axis=1,
    )
    skip_terms = jnp.sum(upstream * product, axis=0)
    tap_total, skip_total = lax.psum((tap_terms, skip_terms), ("outer", "inner"))
    factor = 1.0 / math.sqrt(row_count * devices)
    return (gated_output, stream_grads, longs[2] * factor, tap_total * factor, skip_total * factor)


LANES = 128


def halves(table):
    high = table.astype(ml_dtypes.bfloat16)
    low = (table - high.astype(np.float64)).astype(ml_dtypes.bfloat16)
    return high, low


def fourier_tables(devices, pieces):
    outer_size = devices * pieces
    length = outer_size * LANES
    place = np.arange(outer_size)
    place = (place % devices) * pieces + place // devices
    low = np.arange(outer_size)
    lane = np.arange(LANES)
    angle = 2.0 * np.pi / (4 * outer_size) * ((4 * low[:, None] + 1) * place[None, :] % (4 * outer_size))
    rows = np.concatenate([np.cos(angle), -np.sin(angle)], axis=0)
    row_high, row_low = halves(rows)
    forward_rows = np.concatenate([row_high, row_low, row_high], axis=1)
    back_high, back_low = halves(rows.T / length)
    inverse_rows = np.concatenate([back_high, back_low, back_high], axis=1)
    turn = 2.0 * np.pi / (4 * length) * ((4 * low[:, None] + 1) * lane[None, :] % (4 * length))
    twiddle = np.stack([np.cos(turn), -np.sin(turn)]).astype(np.float32)
    angle = 2.0 * np.pi / LANES * (lane[:, None] * lane[None, :] % LANES)
    cosine, sine = np.cos(angle), -np.sin(angle)
    forward = np.block([[cosine, sine], [-sine, cosine]])
    inverse = np.block([[cosine, -sine], [sine, cosine]])
    columns = np.stack([*halves(forward), *halves(inverse)])
    return forward_rows, inverse_rows, columns, twiddle


def split(value):
    high = value.astype(jnp.bfloat16)
    return high, (value - high.astype(jnp.float32)).astype(jnp.bfloat16)


def dot(left, right):
    return jnp.dot(left, right, preferred_element_type=jnp.float32)


def three_dots(value, high_table, low_table):
    high, low = split(value)
    return dot(high, high_table) + dot(high, low_table) + dot(low, high_table)


def kernel(
    outer_count,
    inner_count,
    query_ref,
    key_ref,
    value_ref,
    taps_ref,
    gain_ref,
    weights_ref,
    cotangent_ref,
    forward_ref,
    inverse_ref,
    columns_ref,
    twiddle_ref,
    gated_ref,
    stream_grads_ref,
    filter_grad_ref,
    tap_grads_ref,
    skip_grad_ref,
    streams,
    mixed,
    product,
    upstream,
    grads,
    sent,
    arrived,
    spectra,
    sent_back,
    arrived_back,
    sums,
    sums_in,
    totals,
    totals_in,
    send_sems,
    recv_sems,
    halo_send,
    halo_recv,
    sum_send,
    sum_recv,
):
    devices = outer_count * inner_count
    row_count = query_ref.shape[0]
    pieces = row_count // LANES
    owned = LANES // devices
    tile = owned * pieces
    outer_size = devices * pieces
    my_outer = lax.axis_index("outer")
    my_inner = lax.axis_index("inner")
    me = my_outer * inner_count + my_inner

    def device(index):
        return (index // inner_count, index % inner_count)

    barrier = pltpu.get_barrier_semaphore()

    def greet(step, carry):
        pl.semaphore_signal(
            barrier, inc=1, device_id=device((me + step) % devices), device_id_type=MESH
        )
        return carry

    lax.fori_loop(1, devices, greet, 0)
    pl.semaphore_wait(barrier, devices - 1)

    following = (me + 1) % devices
    preceding = (me + devices - 1) % devices
    stream_refs = (query_ref, key_ref, value_ref)
    halo_copies = [
        pltpu.make_async_remote_copy(
            src_ref=stream_refs[s].at[pl.ds(row_count - 8, 8), :],
            dst_ref=streams.at[s, pl.ds(0, 8), :],
            send_sem=halo_send.at[s],
            recv_sem=halo_recv.at[s],
            device_id=device(following),
            device_id_type=MESH,
        )
        for s in range(3)
    ]
    for copy in halo_copies:
        copy.start()

    def mine():
        return pl.ds(pl.multiple_of(me * tile, tile), tile)

    def exchange(source, target, group, signal):
        def send(step, carry):
            peer = (me + step) % devices
            pltpu.make_async_remote_copy(
                src_ref=source.at[signal, pl.ds(pl.multiple_of(peer * tile, tile), tile), :],
                dst_ref=target.at[signal, mine(), :],
                send_sem=send_sems.at[group, signal],
                recv_sem=recv_sems.at[group, signal],
                device_id=device(peer),
                device_id_type=MESH,
            ).start()
            return carry

        lax.fori_loop(1, devices, send, 0)
        target[signal, mine(), :] = source[signal, mine(), :]

    def all_but_one(buffer, signal):
        return buffer.at[signal, pl.ds(0, (devices - 1) * tile), :]

    def received(target, group, signal):
        view = all_but_one(target, signal)
        pltpu.make_async_copy(view, view, recv_sems.at[group, signal]).wait()

    def drained(source, group, signal):
        view = all_but_one(source, signal)
        pltpu.make_async_copy(view, view, send_sems.at[group, signal]).wait()

    def put(block, signal, piece):
        sent[signal, pl.ds(piece, LANES, stride=pieces), :] = block.T

    for piece in range(pieces):
        put(taps_ref[pl.ds(piece * LANES, LANES), :], 0, piece)
    exchange(sent, arrived, 0, 0)

    for s in range(3):
        streams[s, pl.ds(8, row_count), :] = stream_refs[s][...]
    for copy in halo_copies:
        copy.wait()
    for s in range(3):
        streams[s, pl.ds(0, 8), :] = jnp.where(me > 0, streams[s, pl.ds(0, 8), :], 0.0)
    def mix(s, piece):
        base = 8 + piece * LANES
        return (
            weights_ref[s, 0:1, :] * streams[s, pl.ds(base, LANES), :]
            + weights_ref[s, 1:2, :] * streams[s, pl.ds(base - 1, LANES), :]
            + weights_ref[s, 2:3, :] * streams[s, pl.ds(base - 2, LANES), :]
        )

    for piece in range(pieces):
        rows = pl.ds(piece * LANES, LANES)
        key, value = mix(1, piece), mix(2, piece)
        mixed[1, rows, :] = key
        mixed[2, rows, :] = value
        product[rows, :] = key * value
        put(key * value, 1, piece)
    exchange(sent, arrived, 0, 1)
    skip_sum = jnp.zeros((1, LANES), jnp.float32)
    for piece in range(pieces):
        rows = pl.ds(piece * LANES, LANES)
        query = mix(0, piece)
        mixed[0, rows, :] = query
        rising = cotangent_ref[rows, :] * query
        upstream[rows, :] = rising
        put(rising, 2, piece)
        skip_sum += jnp.sum(rising * product[rows, :], axis=0, keepdims=True)
    exchange(sent, arrived, 0, 2)

    twiddle_real = twiddle_ref[0]
    twiddle_imag = twiddle_ref[1]

    def transform(signal):
        received(arrived, 0, signal)
        for c in range(owned):
            block = jnp.concatenate(
                [
                    arrived[signal, pl.ds(c * pieces + piece, devices, stride=tile), :]
                    for piece in range(pieces)
                ],
                axis=0,
            )
            high, low = split(block)
            first = dot(forward_ref[...], jnp.concatenate([high, high, low], axis=0))
            real, imag = first[:outer_size], first[outer_size:]
            turned_block = jnp.concatenate(
                [
                    real * twiddle_real - imag * twiddle_imag,
                    real * twiddle_imag + imag * twiddle_real,
                ],
                axis=1,
            )
            spectra[signal, c] = three_dots(turned_block, columns_ref[0], columns_ref[1])

    def back(first, second, conjugated, signal):
        for c in range(owned):
            one, two = spectra[first, c], spectra[second, c]
            one_real, one_imag = one[:, :LANES], one[:, LANES:]
            two_real, two_imag = two[:, :LANES], two[:, LANES:]
            if conjugated:
                real = one_real * two_real + one_imag * two_imag
                imag = one_real * two_imag - one_imag * two_real
            else:
                real = one_real * two_real - one_imag * two_imag
                imag = one_real * two_imag + one_imag * two_real
            inner = three_dots(
                jnp.concatenate([real, imag], axis=1), columns_ref[2], columns_ref[3]
            )
            real, imag = inner[:, :LANES], inner[:, LANES:]
            turned_block = jnp.concatenate(
                [
                    real * twiddle_real + imag * twiddle_imag,
                    imag * twiddle_real - real * twiddle_imag,
                ],
                axis=0,
            )
            high, low = split(turned_block)
            block = dot(inverse_ref[...], jnp.concatenate([high, high, low], axis=0))
            for piece in range(pieces):
                sent_back[signal, pl.ds(c * pieces + piece, devices, stride=tile), :] = block[
                    piece * devices : (piece + 1) * devices
                ]
        exchange(sent_back, arrived_back, 1, signal)

    transform(0)
    transform(1)
    back(0, 1, False, 0)
    transform(2)
    back(0, 2, True, 1)
    back(1, 2, True, 2)

    def piece_of(signal, piece):
        return arrived_back[signal, pl.ds(piece, LANES, stride=pieces), :].T

    gain = gain_ref[...]
    tap_sums = [[jnp.zeros((1, LANES), jnp.float32) for _ in range(3)] for _ in range(3)]

    def add_taps(s, piece, values):
        for j in range(3):
            earlier = streams[s, pl.ds(8 + piece * LANES - j, LANES), :]
            tap_sums[s][j] += jnp.sum(values * earlier, axis=0, keepdims=True)

    received(arrived_back, 1, 0)
    for piece in range(pieces):
        rows = pl.ds(piece * LANES, LANES)
        summed = piece_of(0, piece) + gain * product[rows, :]
        gated_ref[rows, :] = mixed[0, rows, :] * summed
        values = cotangent_ref[rows, :] * summed
        grads[0, rows, :] = values
        add_taps(0, piece, values)
    received(arrived_back, 1, 1)
    for piece in range(pieces):
        rows = pl.ds(piece * LANES, LANES)
        backward = piece_of(1, piece) + gain * upstream[rows, :]
        for s in (1, 2):
            values = backward * mixed[3 - s, rows, :]
            grads[s, rows, :] = values
            add_taps(s, piece, values)

    grad_halo = pltpu.make_async_remote_copy(
        src_ref=grads.at[:, pl.ds(0, 8), :],
        dst_ref=grads.at[:, pl.ds(row_count, 8), :],
        send_sem=halo_send.at[3],
        recv_sem=halo_recv.at[3],
        device_id=device(preceding),
        device_id_type=MESH,
    )
    grad_halo.start()

    group = 4 if inner_count % 4 == 0 else inner_count
    places = inner_count // group
    planes = outer_count * group
    my_place = my_inner // group
    my_member = my_outer * group + my_inner % group
    listed = [tap_sums[s][j] for s in range(3) for j in range(3)] + [skip_sum]
    for at, row in enumerate(listed):
        sums[at : at + 1, :] = row
    sums[10:16, :] = jnp.zeros((6, LANES), jnp.float32)
    sums_in[my_member] = sums[...]

    def send_sums(step, carry):
        member = (my_member + step) % planes
        pltpu.make_async_remote_copy(
            src_ref=sums,
            dst_ref=sums_in.at[my_member],
            send_sem=sum_send.at[0],
            recv_sem=sum_recv.at[0],
            device_id=(member // group, my_place * group + member % group),
            device_id_type=MESH,
        ).start()
        return carry

    lax.fori_loop(1, planes, send_sums, 0)

    def stream_grad(s, start, size):
        return (
            weights_ref[s, 0:1, :] * grads[s, pl.ds(start, size), :]
            + weights_ref[s, 1:2, :] * grads[s, pl.ds(start + 1, size), :]
            + weights_ref[s, 2:3, :] * grads[s, pl.ds(start + 2, size), :]
        )

    for s in range(3):
        for start in range(0, row_count, LANES):
            size = min(LANES, row_count - 8 - start)
            stream_grads_ref[s, pl.ds(start, size), :] = stream_grad(s, start, size)

    def take(view, semaphore):
        pltpu.make_async_copy(view, view, semaphore).wait()

    take(sums_in.at[pl.ds(0, planes - 1)], sum_recv.at[0])
    total = sums_in[0]
    for member in range(1, planes):
        total += sums_in[member]
    totals[...] = total
    totals_in[my_place] = total

    def send_totals(step, carry):
        place = (my_place + step) % places
        pltpu.make_async_remote_copy(
            src_ref=totals,
            dst_ref=totals_in.at[my_place],
            send_sem=sum_send.at[1],
            recv_sem=sum_recv.at[1],
            device_id=(my_outer, place * group + my_inner % group),
            device_id_type=MESH,
        ).start()
        return carry

    lax.fori_loop(1, places, send_totals, 0)

    grad_halo.wait()
    grads[:, pl.ds(row_count, 8), :] = jnp.where(
        me < devices - 1, grads[:, pl.ds(row_count, 8), :], 0.0
    )
    for s in range(3):
        stream_grads_ref[s, pl.ds(row_count - 8, 8), :] = stream_grad(s, row_count - 8, 8)

    factor = 1.0 / math.sqrt(row_count * devices)
    received(arrived_back, 1, 2)
    for piece in range(pieces):
        filter_grad_ref[pl.ds(piece * LANES, LANES), :] = piece_of(2, piece) * factor

    if places > 1:
        take(totals_in.at[pl.ds(0, places - 1)], sum_recv.at[1])
    total = totals_in[0]
    for place in range(1, places):
        total += totals_in[place]
    total = total * factor
    for s in range(3):
        tap_grads_ref[s] = total[3 * s : 3 * s + 3, :]
    skip_grad_ref[...] = total[9:10, :]

    for signal in range(3):
        drained(sent, 0, signal)
        drained(sent_back, 1, signal)
    take(sums_in.at[pl.ds(0, planes - 1)], sum_send.at[0])
    if places > 1:
        take(totals_in.at[pl.ds(0, places - 1)], sum_send.at[1])


def by_channel(
    outer_count,
    inner_count,
    query_stream,
    key_stream,
    value_stream,
    filter_taps,
    skip_gain,
    short_weights,
    cotangent,
):
    row_count, channels = query_stream.shape
    devices = outer_count * inner_count
    pieces = row_count // LANES
    owned = channels // devices
    tables = fourier_tables(devices, pieces)
    group = 4 if inner_count % 4 == 0 else inner_count
    whole = pltpu.VMEM((row_count, channels), jnp.float32)
    three = pltpu.VMEM((3, row_count, channels), jnp.float32)
    padded = pltpu.VMEM((3, row_count + 8, channels), jnp.float32)
    vmem = pl.BlockSpec(memory_space=pltpu.VMEM)
    outs = pl.pallas_call(
        functools.partial(kernel, outer_count, inner_count),
        out_shape=(
            jax.ShapeDtypeStruct((row_count, channels), jnp.float32),
            jax.ShapeDtypeStruct((3, row_count, channels), jnp.float32),
            jax.ShapeDtypeStruct((row_count, channels), jnp.float32),
            jax.ShapeDtypeStruct((3, 3, channels), jnp.float32),
            jax.ShapeDtypeStruct((1, channels), jnp.float32),
        ),
        in_specs=[vmem] * 11,
        out_specs=(vmem,) * 5,
        scratch_shapes=[
            padded,
            three,
            whole,
            whole,
            padded,
            three,
            three,
            pltpu.VMEM((3, owned, devices * pieces, 2 * LANES), jnp.float32),
            three,
            three,
            pltpu.VMEM((16, channels), jnp.float32),
            pltpu.VMEM((outer_count * group, 16, channels), jnp.float32),
            pltpu.VMEM((16, channels), jnp.float32),
            pltpu.VMEM((inner_count // group, 16, channels), jnp.float32),
            pltpu.SemaphoreType.DMA((2, 3)),
            pltpu.SemaphoreType.DMA((2, 3)),
            pltpu.SemaphoreType.DMA((4,)),
            pltpu.SemaphoreType.DMA((4,)),
            pltpu.SemaphoreType.DMA((2,)),
            pltpu.SemaphoreType.DMA((2,)),
        ],
        compiler_params=pltpu.CompilerParams(
            collective_id=0, has_side_effects=True, vmem_limit_bytes=48 * 1024 * 1024
        ),
    )(
        query_stream,
        key_stream,
        value_stream,
        filter_taps,
        skip_gain.reshape(1, channels),
        short_weights,
        cotangent,
        *(jnp.asarray(table) for table in tables),
    )
    return (*outs[:4], outs[4].reshape(channels))


def either_plan(outer_count, inner_count, query_stream, *others):
    row_count, channels = query_stream.shape
    devices = outer_count * inner_count
    even = (
        channels == LANES
        and row_count % LANES == 0
        and channels % devices == 0
        and (channels // devices) * (row_count // LANES) % 8 == 0
        and devices % 8 == 0
    )
    if even:
        return by_channel(outer_count, inner_count, query_stream, *others)
    return on_device(query_stream, *others)


def solution(mesh):
    placed = (
        P(("outer", "inner"), None),
        P(("outer", "inner"), None),
        P(("outer", "inner"), None),
        P(("outer", "inner"), None),
        P(),
        P(),
        P(("outer", "inner"), None),
    )
    return jax.shard_map(
        functools.partial(either_plan, mesh.shape["outer"], mesh.shape["inner"]),
        mesh=mesh,
        in_specs=placed,
        out_specs=(
            P(("outer", "inner"), None),
            P(None, ("outer", "inner"), None),
            P(("outer", "inner"), None),
            P(),
            P(),
        ),
        check_vma=False,
    )
```

```python
import functools
import math

import jax
import jax.numpy as jnp
import ml_dtypes
import numpy as np
from jax import lax
from jax.experimental import pallas as pl
from jax.experimental.pallas import tpu as pltpu
from jax.sharding import PartitionSpec as P

MESH = pl.DeviceIdType.MESH

exact_mode = lax.Precision.HIGHEST


def passed_along(block, axis, distance):
    devices = range(lax.axis_size(axis))
    route = [(i - distance, i) for i in devices if i - distance in devices]
    return lax.ppermute(block, axis, route)


def unit_angles(counts_table, period):
    return 2.0 * math.pi / period * (counts_table % period).astype(jnp.float32)


def turned(real_part, imag_part, cosine, sine, sign):
    return (
        real_part * cosine - sign * imag_part * sine,
        imag_part * cosine + sign * real_part * sine,
    )


def applied(formula, angles, real_part, imag_part, sign):
    cosine = jnp.cos(angles)
    sine = jnp.sin(angles)
    cos_real = jnp.einsum(formula, cosine, real_part, precision=exact_mode)
    cos_imag = jnp.einsum(formula, cosine, imag_part, precision=exact_mode)
    sin_real = jnp.einsum(formula, sine, real_part, precision=exact_mode)
    sin_imag = jnp.einsum(formula, sine, imag_part, precision=exact_mode)
    return (cos_real - sign * sin_imag, cos_imag + sign * sin_real)


def sequence_blocks(tiles):
    groups, devices, tile_size = tiles.shape
    shaped = tiles.reshape(groups, lax.axis_size("outer"), lax.axis_size("inner"), 1, 1, tile_size)
    moved = lax.all_to_all(
        lax.all_to_all(shaped, "outer", split_axis=1, concat_axis=3, tiled=True),
        "inner",
        split_axis=2,
        concat_axis=4,
        tiled=True,
    )
    return moved.reshape(groups, devices, tile_size)


def spectral_blocks(tiles):
    groups, devices, tile_size = tiles.shape
    shaped = tiles.reshape(groups, lax.axis_size("outer"), lax.axis_size("inner"), 1, 1, tile_size)
    moved = lax.all_to_all(
        lax.all_to_all(shaped, "outer", split_axis=1, concat_axis=3, tiled=True),
        "inner",
        split_axis=2,
        concat_axis=4,
        tiled=True,
    )
    return moved.reshape(groups, devices, tile_size)


def self_position():
    return lax.axis_index("outer") * lax.axis_size("inner") + lax.axis_index("inner")


def local_forward(real_part, imag_part):
    members, pairs, row_count, channels = real_part.shape
    second = row_count // 16
    first_index = jnp.arange(16, dtype=jnp.int32)
    second_index = jnp.arange(second, dtype=jnp.int32)
    real_part = real_part.reshape(members, pairs, 16, second, channels)
    imag_part = imag_part.reshape(members, pairs, 16, second, channels)
    first_angles = unit_angles(first_index[:, None] * first_index[None, :], 16)
    real_part, imag_part = applied("ka,mtacx->mtkcx", first_angles, real_part, imag_part, -1.0)
    twiddle = unit_angles(first_index[:, None] * second_index[None, :], row_count)[:, :, None]
    real_part, imag_part = turned(real_part, imag_part, jnp.cos(twiddle), jnp.sin(twiddle), -1.0)
    second_angles = unit_angles(second_index[:, None] * second_index[None, :], second)
    real_part, imag_part = applied("qc,mtkcx->mtqkx", second_angles, real_part, imag_part, -1.0)
    return (
        real_part.reshape(members, pairs, row_count, channels),
        imag_part.reshape(members, pairs, row_count, channels),
    )


def local_inverse(real_part, imag_part):
    members, pairs, row_count, channels = real_part.shape
    second = row_count // 16
    first_index = jnp.arange(16, dtype=jnp.int32)
    second_index = jnp.arange(second, dtype=jnp.int32)
    real_part = real_part.reshape(members, pairs, second, 16, channels)
    imag_part = imag_part.reshape(members, pairs, second, 16, channels)
    second_angles = unit_angles(second_index[:, None] * second_index[None, :], second)
    real_part, imag_part = applied("cq,mtqkx->mtckx", second_angles, real_part, imag_part, 1.0)
    twiddle = unit_angles(second_index[:, None] * first_index[None, :], row_count)[:, :, None]
    real_part, imag_part = turned(real_part, imag_part, jnp.cos(twiddle), jnp.sin(twiddle), 1.0)
    first_angles = unit_angles(first_index[:, None] * first_index[None, :], 16)
    real_part, imag_part = applied("ak,mtckx->mtacx", first_angles, real_part, imag_part, 1.0)
    return (
        real_part.reshape(members, pairs, row_count, channels),
        imag_part.reshape(members, pairs, row_count, channels),
    )


def fourier_forward(signals):
    members, row_count, channels = signals.shape
    devices = lax.axis_size("outer") * lax.axis_size("inner")
    tile_rows = row_count // devices
    length = 2 * row_count * devices
    columns = sequence_blocks(signals.reshape(members, devices, tile_rows * channels))
    parity = jnp.arange(2, dtype=jnp.int32)
    target = jnp.arange(devices, dtype=jnp.int32)
    frequency = 2 * target[None, :] + parity[:, None]
    angles = unit_angles(frequency[:, :, None] * target[None, None, :], 2 * devices)
    first_real = jnp.einsum("tdb,mbx->mtdx", jnp.cos(angles), columns, precision=exact_mode)
    first_imag = -jnp.einsum("tdb,mbx->mtdx", jnp.sin(angles), columns, precision=exact_mode)
    first_real = first_real.reshape(members, 2, devices, tile_rows, channels)
    first_imag = first_imag.reshape(members, 2, devices, tile_rows, channels)
    offset = self_position() * tile_rows + jnp.arange(tile_rows, dtype=jnp.int32)
    twiddle = unit_angles(frequency[:, :, None] * offset[None, None, :], length)[:, :, :, None]
    first_real, first_imag = turned(
        first_real, first_imag, jnp.cos(twiddle), jnp.sin(twiddle), -1.0
    )
    stacked = jnp.stack([first_real, first_imag], axis=1).reshape(
        members * 4, devices, tile_rows * channels
    )
    spread = spectral_blocks(stacked).reshape(members, 2, 2, row_count, channels)
    return local_forward(spread[:, 0], spread[:, 1])


def fourier_inverse(real_part, imag_part):
    members, pairs, row_count, channels = real_part.shape
    devices = lax.axis_size("outer") * lax.axis_size("inner")
    tile_rows = row_count // devices
    length = 2 * row_count * devices
    real_part, imag_part = local_inverse(real_part, imag_part)
    parity = jnp.arange(2, dtype=jnp.int32)
    frequency = 2 * self_position() + parity
    twiddle = unit_angles(
        frequency[:, None] * jnp.arange(row_count, dtype=jnp.int32)[None, :], length
    )[:, :, None]
    real_part, imag_part = turned(real_part, imag_part, jnp.cos(twiddle), jnp.sin(twiddle), 1.0)
    stacked = jnp.stack([real_part, imag_part], axis=1).reshape(
        members * 4, devices, tile_rows * channels
    )
    gathered = spectral_blocks(stacked).reshape(members, 2, 2, devices, tile_rows * channels)
    target = jnp.arange(devices, dtype=jnp.int32)
    angles = unit_angles(
        target[:, None, None] * (2 * target[None, None, :] + parity[None, :, None]), 2 * devices
    )
    cosine = jnp.cos(angles)
    sine = jnp.sin(angles)
    scale = 1.0 / length
    real_out = (
        jnp.einsum("btd,mtdx->mbx", cosine, gathered[:, 0], precision=exact_mode)
        - jnp.einsum("btd,mtdx->mbx", sine, gathered[:, 1], precision=exact_mode)
    ) * scale
    imag_out = real_out[:0]
    return (real_out, imag_out)


def on_device(
    query_stream, key_stream, value_stream, filter_taps, skip_gain, short_weights, cotangent
):
    row_count, channels = query_stream.shape
    devices = lax.axis_size("outer") * lax.axis_size("inner")
    streams = jnp.stack([query_stream, key_stream, value_stream])
    earlier = passed_along(streams[:, row_count - 2 :, :], ("outer", "inner"), 1)
    ahead = jnp.concatenate([earlier, streams], axis=1)
    lag_one = ahead[:, 1 : row_count + 1]
    lag_two = ahead[:, 0:row_count]
    mixed = (
        short_weights[:, 0:1] * streams
        + short_weights[:, 1:2] * lag_one
        + short_weights[:, 2:3] * lag_two
    )
    product = mixed[1] * mixed[2]
    upstream = cotangent * mixed[0]
    spec_real, spec_imag = fourier_forward(jnp.stack([filter_taps, product, upstream]))
    filter_real, product_real, upstream_real = (spec_real[0], spec_real[1], spec_real[2])
    filter_imag, product_imag, upstream_imag = (spec_imag[0], spec_imag[1], spec_imag[2])
    causal_real = filter_real * product_real - filter_imag * product_imag
    causal_imag = filter_real * product_imag + filter_imag * product_real
    back_real = filter_real * upstream_real + filter_imag * upstream_imag
    back_imag = filter_real * upstream_imag - filter_imag * upstream_real
    grad_real = product_real * upstream_real + product_imag * upstream_imag
    grad_imag = product_real * upstream_imag - product_imag * upstream_real
    real_out, imag_out = fourier_inverse(
        jnp.stack([causal_real, back_real, grad_real]),
        jnp.stack([causal_imag, back_imag, grad_imag]),
    )
    longs = sequence_blocks(real_out).reshape(3, row_count, channels)
    summed = longs[0] + skip_gain * product
    gated_output = mixed[0] * summed
    backward = longs[1] + skip_gain * upstream
    grads = jnp.stack([cotangent * summed, backward * mixed[2], backward * mixed[1]])
    later = passed_along(grads[:, 0:2, :], ("outer", "inner"), -1)
    behind = jnp.concatenate([grads, later], axis=1)
    stream_grads = (
        short_weights[:, 0:1] * grads
        + short_weights[:, 1:2] * behind[:, 1 : row_count + 1]
        + short_weights[:, 2:3] * behind[:, 2 : row_count + 2]
    )
    tap_terms = jnp.stack(
        [
            jnp.sum(grads * streams, axis=1),
            jnp.sum(grads * lag_one, axis=1),
            jnp.sum(grads * lag_two, axis=1),
        ],
        axis=1,
    )
    skip_terms = jnp.sum(upstream * product, axis=0)
    tap_total, skip_total = lax.psum((tap_terms, skip_terms), ("outer", "inner"))
    factor = 1.0 / math.sqrt(row_count * devices)
    return (gated_output, stream_grads, longs[2] * factor, tap_total * factor, skip_total * factor)


LANES = 128


def halves(table):
    high = table.astype(ml_dtypes.bfloat16)
    low = (table - high.astype(np.float64)).astype(ml_dtypes.bfloat16)
    return high, low


def fourier_tables(devices, pieces):
    outer_size = devices * pieces
    length = outer_size * LANES
    place = np.arange(outer_size)
    place = (place % devices) * pieces + place // devices
    low = np.arange(outer_size)
    lane = np.arange(LANES)
    angle = 2.0 * np.pi / (4 * outer_size) * ((4 * low[:, None] + 1) * place[None, :] % (4 * outer_size))
    rows = np.concatenate([np.cos(angle), -np.sin(angle)], axis=0)
    row_high, row_low = halves(rows)
    forward_rows = np.concatenate([row_high, row_low, row_high], axis=1)
    back_high, back_low = halves(rows.T / length)
    inverse_rows = np.concatenate([back_high, back_low, back_high], axis=1)
    turn = 2.0 * np.pi / (4 * length) * ((4 * low[:, None] + 1) * lane[None, :] % (4 * length))
    twiddle = np.stack([np.cos(turn), -np.sin(turn)]).astype(np.float32)
    angle = 2.0 * np.pi / LANES * (lane[:, None] * lane[None, :] % LANES)
    cosine, sine = np.cos(angle), -np.sin(angle)
    forward = np.block([[cosine, sine], [-sine, cosine]])
    inverse = np.block([[cosine, -sine], [sine, cosine]])
    columns = np.stack([*halves(forward), *halves(inverse)])
    return forward_rows, inverse_rows, columns, twiddle


def split(value):
    high = value.astype(jnp.bfloat16)
    return high, (value - high.astype(jnp.float32)).astype(jnp.bfloat16)


def dot(left, right):
    return jnp.dot(left, right, preferred_element_type=jnp.float32)


def three_dots(value, high_table, low_table):
    high, low = split(value)
    return dot(high, high_table) + dot(high, low_table) + dot(low, high_table)


def kernel(
    outer_count,
    inner_count,
    query_hbm,
    key_hbm,
    value_hbm,
    taps_hbm,
    gain_hbm,
    weights_hbm,
    cotangent_hbm,
    forward_hbm,
    inverse_hbm,
    columns_hbm,
    twiddle_hbm,
    gated_ref,
    stream_grads_ref,
    filter_grad_ref,
    tap_grads_ref,
    skip_grad_ref,
    streams,
    mixed,
    product,
    upstream,
    grads,
    sent,
    arrived,
    spectra,
    sent_back,
    arrived_back,
    sums,
    sums_in,
    totals,
    totals_in,
    send_sems,
    recv_sems,
    halo_send,
    halo_recv,
    sum_send,
    sum_recv,
    taps_ref,
    gain_ref,
    weights_ref,
    cotangent_ref,
    forward_ref,
    inverse_ref,
    columns_ref,
    twiddle_ref,
    load_sems,
):
    devices = outer_count * inner_count
    row_count = query_hbm.shape[0]
    pieces = row_count // LANES
    owned = LANES // devices
    tile = owned * pieces
    outer_size = devices * pieces
    my_outer = lax.axis_index("outer")
    my_inner = lax.axis_index("inner")
    me = my_outer * inner_count + my_inner

    def device(index):
        return (index // inner_count, index % inner_count)

    barrier = pltpu.get_barrier_semaphore()

    def greet(step, carry):
        pl.semaphore_signal(
            barrier, inc=1, device_id=device((me + step) % devices), device_id_type=MESH
        )
        return carry

    lax.fori_loop(1, devices, greet, 0)

    stream_hbms = (query_hbm, key_hbm, value_hbm)
    loads = {}
    for at, (name, source, target) in enumerate(
        [
            ("taps", taps_hbm, taps_ref),
            ("key", key_hbm, streams.at[1, pl.ds(8, row_count), :]),
            ("value", value_hbm, streams.at[2, pl.ds(8, row_count), :]),
            ("query", query_hbm, streams.at[0, pl.ds(8, row_count), :]),
            ("weights", weights_hbm, weights_ref),
            ("cotangent", cotangent_hbm, cotangent_ref),
            ("forward", forward_hbm, forward_ref),
            ("twiddle", twiddle_hbm, twiddle_ref),
            ("columns", columns_hbm, columns_ref),
            ("inverse", inverse_hbm, inverse_ref),
            ("gain", gain_hbm, gain_ref),
        ]
    ):
        loads[name] = pltpu.make_async_copy(source, target, load_sems.at[at])
        loads[name].start()

    following = (me + 1) % devices
    preceding = (me + devices - 1) % devices
    halo_copies = [
        pltpu.make_async_remote_copy(
            src_ref=stream_hbms[s].at[pl.ds(row_count - 8, 8), :],
            dst_ref=streams.at[s, pl.ds(0, 8), :],
            send_sem=halo_send.at[s],
            recv_sem=halo_recv.at[s],
            device_id=device(following),
            device_id_type=MESH,
        )
        for s in range(3)
    ]

    group = 4 if inner_count % 4 == 0 else inner_count
    places = inner_count // group
    planes = outer_count * group
    my_place = my_inner // group
    my_member = my_outer * group + my_inner % group

    def peer_at(step):
        place = (my_place + places - step % places) % places
        turn = ((step - 1) // places + 1) % planes
        outer = (my_outer + turn) % outer_count
        member = (my_inner + turn // outer_count) % group
        return outer * inner_count + place * group + member

    def mine():
        return pl.ds(pl.multiple_of(me * tile, tile), tile)

    def exchange(source, target, group, signal):
        def send(step, carry):
            peer = peer_at(step)
            pltpu.make_async_remote_copy(
                src_ref=source.at[signal, pl.ds(pl.multiple_of(peer * tile, tile), tile), :],
                dst_ref=target.at[signal, mine(), :],
                send_sem=send_sems.at[group, signal],
                recv_sem=recv_sems.at[group, signal],
                device_id=device(peer),
                device_id_type=MESH,
            ).start()
            return carry

        lax.fori_loop(1, devices, send, 0)
        target[signal, mine(), :] = source[signal, mine(), :]

    def all_but_one(buffer, signal):
        return buffer.at[signal, pl.ds(0, (devices - 1) * tile), :]

    def received(target, group, signal):
        view = all_but_one(target, signal)
        pltpu.make_async_copy(view, view, recv_sems.at[group, signal]).wait()

    def drained(source, group, signal):
        view = all_but_one(source, signal)
        pltpu.make_async_copy(view, view, send_sems.at[group, signal]).wait()

    def put(block, signal, piece):
        sent[signal, pl.ds(piece, LANES, stride=pieces), :] = block.T

    loads["taps"].wait()
    for piece in range(pieces):
        put(taps_ref[pl.ds(piece * LANES, LANES), :], 0, piece)
    pl.semaphore_wait(barrier, devices - 1)

    for copy in halo_copies:
        copy.start()
    exchange(sent, arrived, 0, 0)

    for name in ("key", "value", "query", "weights", "cotangent"):
        loads[name].wait()
    for copy in halo_copies:
        copy.wait()
    for s in range(3):
        streams[s, pl.ds(0, 8), :] = jnp.where(me > 0, streams[s, pl.ds(0, 8), :], 0.0)

    def mix(s, piece):
        base = 8 + piece * LANES
        return (
            weights_ref[s, 0:1, :] * streams[s, pl.ds(base, LANES), :]
            + weights_ref[s, 1:2, :] * streams[s, pl.ds(base - 1, LANES), :]
            + weights_ref[s, 2:3, :] * streams[s, pl.ds(base - 2, LANES), :]
        )

    for piece in range(pieces):
        rows = pl.ds(piece * LANES, LANES)
        key, value = mix(1, piece), mix(2, piece)
        mixed[1, rows, :] = key
        mixed[2, rows, :] = value
        product[rows, :] = key * value
        put(key * value, 1, piece)
    exchange(sent, arrived, 0, 1)
    skip_sum = jnp.zeros((1, LANES), jnp.float32)
    for piece in range(pieces):
        rows = pl.ds(piece * LANES, LANES)
        query = mix(0, piece)
        mixed[0, rows, :] = query
        rising = cotangent_ref[rows, :] * query
        upstream[rows, :] = rising
        put(rising, 2, piece)
        skip_sum += jnp.sum(rising * product[rows, :], axis=0, keepdims=True)
    exchange(sent, arrived, 0, 2)

    for name in ("forward", "twiddle", "columns", "inverse", "gain"):
        loads[name].wait()
    twiddle_real = twiddle_ref[0]
    twiddle_imag = twiddle_ref[1]

    def transform(signal):
        received(arrived, 0, signal)
        for c in range(owned):
            block = jnp.concatenate(
                [
                    arrived[signal, pl.ds(c * pieces + piece, devices, stride=tile), :]
                    for piece in range(pieces)
                ],
                axis=0,
            )
            high, low = split(block)
            first = dot(forward_ref[...], jnp.concatenate([high, high, low], axis=0))
            real, imag = first[:outer_size], first[outer_size:]
            turned_block = jnp.concatenate(
                [
                    real * twiddle_real - imag * twiddle_imag,
                    real * twiddle_imag + imag * twiddle_real,
                ],
                axis=1,
            )
            spectra[signal, c] = three_dots(turned_block, columns_ref[0], columns_ref[1])

    def back(first, second, conjugated, signal):
        for c in range(owned):
            one, two = spectra[first, c], spectra[second, c]
            one_real, one_imag = one[:, :LANES], one[:, LANES:]
            two_real, two_imag = two[:, :LANES], two[:, LANES:]
            if conjugated:
                real = one_real * two_real + one_imag * two_imag
                imag = one_real * two_imag - one_imag * two_real
            else:
                real = one_real * two_real - one_imag * two_imag
                imag = one_real * two_imag + one_imag * two_real
            inner = three_dots(
                jnp.concatenate([real, imag], axis=1), columns_ref[2], columns_ref[3]
            )
            real, imag = inner[:, :LANES], inner[:, LANES:]
            turned_block = jnp.concatenate(
                [
                    real * twiddle_real + imag * twiddle_imag,
                    imag * twiddle_real - real * twiddle_imag,
                ],
                axis=0,
            )
            high, low = split(turned_block)
            block = dot(inverse_ref[...], jnp.concatenate([high, high, low], axis=0))
            for piece in range(pieces):
                sent_back[signal, pl.ds(c * pieces + piece, devices, stride=tile), :] = block[
                    piece * devices : (piece + 1) * devices
                ]
        exchange(sent_back, arrived_back, 1, signal)

    transform(0)
    transform(1)
    back(0, 1, False, 0)
    transform(2)
    back(0, 2, True, 1)
    back(1, 2, True, 2)

    def piece_of(signal, piece):
        return arrived_back[signal, pl.ds(piece, LANES, stride=pieces), :].T

    gain = gain_ref[...]
    tap_sums = [[jnp.zeros((1, LANES), jnp.float32) for _ in range(3)] for _ in range(3)]

    def add_taps(s, piece, values):
        for j in range(3):
            earlier = streams[s, pl.ds(8 + piece * LANES - j, LANES), :]
            tap_sums[s][j] += jnp.sum(values * earlier, axis=0, keepdims=True)

    received(arrived_back, 1, 0)
    for piece in range(pieces):
        rows = pl.ds(piece * LANES, LANES)
        summed = piece_of(0, piece) + gain * product[rows, :]
        gated_ref[rows, :] = mixed[0, rows, :] * summed
        values = cotangent_ref[rows, :] * summed
        grads[0, rows, :] = values
        add_taps(0, piece, values)
    received(arrived_back, 1, 1)
    for piece in range(pieces):
        rows = pl.ds(piece * LANES, LANES)
        backward = piece_of(1, piece) + gain * upstream[rows, :]
        for s in (1, 2):
            values = backward * mixed[3 - s, rows, :]
            grads[s, rows, :] = values
            add_taps(s, piece, values)

    grad_halo = pltpu.make_async_remote_copy(
        src_ref=grads.at[:, pl.ds(0, 8), :],
        dst_ref=grads.at[:, pl.ds(row_count, 8), :],
        send_sem=halo_send.at[3],
        recv_sem=halo_recv.at[3],
        device_id=device(preceding),
        device_id_type=MESH,
    )
    grad_halo.start()

    listed = [tap_sums[s][j] for s in range(3) for j in range(3)] + [skip_sum]
    for at, row in enumerate(listed):
        sums[at : at + 1, :] = row
    sums[10:16, :] = jnp.zeros((6, LANES), jnp.float32)
    sums_in[my_member] = sums[...]

    def send_sums(step, carry):
        member = (my_member + step) % planes
        pltpu.make_async_remote_copy(
            src_ref=sums,
            dst_ref=sums_in.at[my_member],
            send_sem=sum_send.at[0],
            recv_sem=sum_recv.at[0],
            device_id=(member // group, my_place * group + member % group),
            device_id_type=MESH,
        ).start()
        return carry

    lax.fori_loop(1, planes, send_sums, 0)

    def stream_grad(s, start, size):
        return (
            weights_ref[s, 0:1, :] * grads[s, pl.ds(start, size), :]
            + weights_ref[s, 1:2, :] * grads[s, pl.ds(start + 1, size), :]
            + weights_ref[s, 2:3, :] * grads[s, pl.ds(start + 2, size), :]
        )

    for s in range(3):
        for start in range(0, row_count, LANES):
            size = min(LANES, row_count - 8 - start)
            stream_grads_ref[s, pl.ds(start, size), :] = stream_grad(s, start, size)

    def take(view, semaphore):
        pltpu.make_async_copy(view, view, semaphore).wait()

    take(sums_in.at[pl.ds(0, planes - 1)], sum_recv.at[0])
    total = sums_in[0]
    for member in range(1, planes):
        total += sums_in[member]
    totals[...] = total
    totals_in[my_place] = total

    def send_totals(step, carry):
        place = (my_place + step) % places
        pltpu.make_async_remote_copy(
            src_ref=totals,
            dst_ref=totals_in.at[my_place],
            send_sem=sum_send.at[1],
            recv_sem=sum_recv.at[1],
            device_id=(my_outer, place * group + my_inner % group),
            device_id_type=MESH,
        ).start()
        return carry

    lax.fori_loop(1, places, send_totals, 0)

    grad_halo.wait()
    grads[:, pl.ds(row_count, 8), :] = jnp.where(
        me < devices - 1, grads[:, pl.ds(row_count, 8), :], 0.0
    )
    for s in range(3):
        stream_grads_ref[s, pl.ds(row_count - 8, 8), :] = stream_grad(s, row_count - 8, 8)

    factor = 1.0 / math.sqrt(row_count * devices)
    received(arrived_back, 1, 2)
    for piece in range(pieces):
        filter_grad_ref[pl.ds(piece * LANES, LANES), :] = piece_of(2, piece) * factor

    if places > 1:
        take(totals_in.at[pl.ds(0, places - 1)], sum_recv.at[1])
    total = totals_in[0]
    for place in range(1, places):
        total += totals_in[place]
    total = total * factor
    for s in range(3):
        tap_grads_ref[s] = total[3 * s : 3 * s + 3, :]
    skip_grad_ref[...] = total[9:10, :]

    for signal in range(3):
        drained(sent, 0, signal)
        drained(sent_back, 1, signal)
    take(sums_in.at[pl.ds(0, planes - 1)], sum_send.at[0])
    if places > 1:
        take(totals_in.at[pl.ds(0, places - 1)], sum_send.at[1])


def store_kernel(*refs):
    sources, targets, sems = refs[:5], refs[5:10], refs[10]
    copies = [
        pltpu.make_async_copy(source, target, sems.at[at])
        for at, (source, target) in enumerate(zip(sources, targets))
    ]
    for copy in copies:
        copy.start()
    for copy in copies:
        copy.wait()


def by_channel(
    outer_count,
    inner_count,
    query_stream,
    key_stream,
    value_stream,
    filter_taps,
    skip_gain,
    short_weights,
    cotangent,
):
    row_count, channels = query_stream.shape
    devices = outer_count * inner_count
    pieces = row_count // LANES
    owned = channels // devices
    tables = fourier_tables(devices, pieces)
    group = 4 if inner_count % 4 == 0 else inner_count
    whole = pltpu.VMEM((row_count, channels), jnp.float32)
    three = pltpu.VMEM((3, row_count, channels), jnp.float32)
    padded = pltpu.VMEM((3, row_count + 8, channels), jnp.float32)
    vmem = pl.BlockSpec(memory_space=pltpu.VMEM)
    outs = pl.pallas_call(
        functools.partial(kernel, outer_count, inner_count),
        out_shape=(
            jax.ShapeDtypeStruct((row_count, channels), jnp.float32),
            jax.ShapeDtypeStruct((3, row_count, channels), jnp.float32),
            jax.ShapeDtypeStruct((row_count, channels), jnp.float32),
            jax.ShapeDtypeStruct((3, 3, channels), jnp.float32),
            jax.ShapeDtypeStruct((1, channels), jnp.float32),
        ),
        in_specs=[pl.BlockSpec(memory_space=pltpu.HBM)] * 11,
        out_specs=(vmem,) * 5,
        scratch_shapes=[
            padded,
            three,
            whole,
            whole,
            padded,
            three,
            three,
            pltpu.VMEM((3, owned, devices * pieces, 2 * LANES), jnp.float32),
            three,
            three,
            pltpu.VMEM((16, channels), jnp.float32),
            pltpu.VMEM((outer_count * group, 16, channels), jnp.float32),
            pltpu.VMEM((16, channels), jnp.float32),
            pltpu.VMEM((inner_count // group, 16, channels), jnp.float32),
            pltpu.SemaphoreType.DMA((2, 3)),
            pltpu.SemaphoreType.DMA((2, 3)),
            pltpu.SemaphoreType.DMA((4,)),
            pltpu.SemaphoreType.DMA((4,)),
            pltpu.SemaphoreType.DMA((2,)),
            pltpu.SemaphoreType.DMA((2,)),
            whole,
            pltpu.VMEM((1, channels), jnp.float32),
            pltpu.VMEM(short_weights.shape, jnp.float32),
            whole,
            *(pltpu.VMEM(table.shape, table.dtype) for table in tables),
            pltpu.SemaphoreType.DMA((11,)),
        ],
        compiler_params=pltpu.CompilerParams(
            collective_id=0, has_side_effects=True, vmem_limit_bytes=63 * 1024 * 1024
        ),
    )(
        query_stream,
        key_stream,
        value_stream,
        filter_taps,
        skip_gain.reshape(1, channels),
        short_weights,
        cotangent,
        *(jnp.asarray(table) for table in tables),
    )
    outs = pl.pallas_call(
        store_kernel,
        out_shape=tuple(jax.ShapeDtypeStruct(out.shape, out.dtype) for out in outs),
        in_specs=[vmem] * 5,
        out_specs=(pl.BlockSpec(memory_space=pltpu.HBM),) * 5,
        scratch_shapes=[pltpu.SemaphoreType.DMA((5,))],
    )(*outs)
    return (*outs[:4], outs[4].reshape(channels))


def either_plan(outer_count, inner_count, query_stream, *others):
    row_count, channels = query_stream.shape
    devices = outer_count * inner_count
    even = (
        channels == LANES
        and row_count % LANES == 0
        and channels % devices == 0
        and (channels // devices) * (row_count // LANES) % 8 == 0
        and devices % 8 == 0
    )
    if even:
        return by_channel(outer_count, inner_count, query_stream, *others)
    return on_device(query_stream, *others)


def solution(mesh):
    placed = (
        P(("outer", "inner"), None),
        P(("outer", "inner"), None),
        P(("outer", "inner"), None),
        P(("outer", "inner"), None),
        P(),
        P(),
        P(("outer", "inner"), None),
    )
    return jax.shard_map(
        functools.partial(either_plan, mesh.shape["outer"], mesh.shape["inner"]),
        mesh=mesh,
        in_specs=placed,
        out_specs=(
            P(("outer", "inner"), None),
            P(None, ("outer", "inner"), None),
            P(("outer", "inner"), None),
            P(),
            P(),
        ),
        check_vma=False,
    )
```

```python
import functools
import math

import jax
import jax.numpy as jnp
import ml_dtypes
import numpy as np
from jax import lax
from jax.experimental import pallas as pl
from jax.experimental.pallas import tpu as pltpu
from jax.sharding import PartitionSpec as P

MESH = pl.DeviceIdType.MESH

exact_mode = lax.Precision.HIGHEST


def passed_along(block, axis, distance):
    devices = range(lax.axis_size(axis))
    route = [(i - distance, i) for i in devices if i - distance in devices]
    return lax.ppermute(block, axis, route)


def unit_angles(counts_table, period):
    return 2.0 * math.pi / period * (counts_table % period).astype(jnp.float32)


def turned(real_part, imag_part, cosine, sine, sign):
    return (
        real_part * cosine - sign * imag_part * sine,
        imag_part * cosine + sign * real_part * sine,
    )


def applied(formula, angles, real_part, imag_part, sign):
    cosine = jnp.cos(angles)
    sine = jnp.sin(angles)
    cos_real = jnp.einsum(formula, cosine, real_part, precision=exact_mode)
    cos_imag = jnp.einsum(formula, cosine, imag_part, precision=exact_mode)
    sin_real = jnp.einsum(formula, sine, real_part, precision=exact_mode)
    sin_imag = jnp.einsum(formula, sine, imag_part, precision=exact_mode)
    return (cos_real - sign * sin_imag, cos_imag + sign * sin_real)


def sequence_blocks(tiles):
    groups, devices, tile_size = tiles.shape
    shaped = tiles.reshape(groups, lax.axis_size("outer"), lax.axis_size("inner"), 1, 1, tile_size)
    moved = lax.all_to_all(
        lax.all_to_all(shaped, "outer", split_axis=1, concat_axis=3, tiled=True),
        "inner",
        split_axis=2,
        concat_axis=4,
        tiled=True,
    )
    return moved.reshape(groups, devices, tile_size)


def spectral_blocks(tiles):
    groups, devices, tile_size = tiles.shape
    shaped = tiles.reshape(groups, lax.axis_size("outer"), lax.axis_size("inner"), 1, 1, tile_size)
    moved = lax.all_to_all(
        lax.all_to_all(shaped, "outer", split_axis=1, concat_axis=3, tiled=True),
        "inner",
        split_axis=2,
        concat_axis=4,
        tiled=True,
    )
    return moved.reshape(groups, devices, tile_size)


def self_position():
    return lax.axis_index("outer") * lax.axis_size("inner") + lax.axis_index("inner")


def local_forward(real_part, imag_part):
    members, pairs, row_count, channels = real_part.shape
    second = row_count // 16
    first_index = jnp.arange(16, dtype=jnp.int32)
    second_index = jnp.arange(second, dtype=jnp.int32)
    real_part = real_part.reshape(members, pairs, 16, second, channels)
    imag_part = imag_part.reshape(members, pairs, 16, second, channels)
    first_angles = unit_angles(first_index[:, None] * first_index[None, :], 16)
    real_part, imag_part = applied("ka,mtacx->mtkcx", first_angles, real_part, imag_part, -1.0)
    twiddle = unit_angles(first_index[:, None] * second_index[None, :], row_count)[:, :, None]
    real_part, imag_part = turned(real_part, imag_part, jnp.cos(twiddle), jnp.sin(twiddle), -1.0)
    second_angles = unit_angles(second_index[:, None] * second_index[None, :], second)
    real_part, imag_part = applied("qc,mtkcx->mtqkx", second_angles, real_part, imag_part, -1.0)
    return (
        real_part.reshape(members, pairs, row_count, channels),
        imag_part.reshape(members, pairs, row_count, channels),
    )


def local_inverse(real_part, imag_part):
    members, pairs, row_count, channels = real_part.shape
    second = row_count // 16
    first_index = jnp.arange(16, dtype=jnp.int32)
    second_index = jnp.arange(second, dtype=jnp.int32)
    real_part = real_part.reshape(members, pairs, second, 16, channels)
    imag_part = imag_part.reshape(members, pairs, second, 16, channels)
    second_angles = unit_angles(second_index[:, None] * second_index[None, :], second)
    real_part, imag_part = applied("cq,mtqkx->mtckx", second_angles, real_part, imag_part, 1.0)
    twiddle = unit_angles(second_index[:, None] * first_index[None, :], row_count)[:, :, None]
    real_part, imag_part = turned(real_part, imag_part, jnp.cos(twiddle), jnp.sin(twiddle), 1.0)
    first_angles = unit_angles(first_index[:, None] * first_index[None, :], 16)
    real_part, imag_part = applied("ak,mtckx->mtacx", first_angles, real_part, imag_part, 1.0)
    return (
        real_part.reshape(members, pairs, row_count, channels),
        imag_part.reshape(members, pairs, row_count, channels),
    )


def fourier_forward(signals):
    members, row_count, channels = signals.shape
    devices = lax.axis_size("outer") * lax.axis_size("inner")
    tile_rows = row_count // devices
    length = 2 * row_count * devices
    columns = sequence_blocks(signals.reshape(members, devices, tile_rows * channels))
    parity = jnp.arange(2, dtype=jnp.int32)
    target = jnp.arange(devices, dtype=jnp.int32)
    frequency = 2 * target[None, :] + parity[:, None]
    angles = unit_angles(frequency[:, :, None] * target[None, None, :], 2 * devices)
    first_real = jnp.einsum("tdb,mbx->mtdx", jnp.cos(angles), columns, precision=exact_mode)
    first_imag = -jnp.einsum("tdb,mbx->mtdx", jnp.sin(angles), columns, precision=exact_mode)
    first_real = first_real.reshape(members, 2, devices, tile_rows, channels)
    first_imag = first_imag.reshape(members, 2, devices, tile_rows, channels)
    offset = self_position() * tile_rows + jnp.arange(tile_rows, dtype=jnp.int32)
    twiddle = unit_angles(frequency[:, :, None] * offset[None, None, :], length)[:, :, :, None]
    first_real, first_imag = turned(
        first_real, first_imag, jnp.cos(twiddle), jnp.sin(twiddle), -1.0
    )
    stacked = jnp.stack([first_real, first_imag], axis=1).reshape(
        members * 4, devices, tile_rows * channels
    )
    spread = spectral_blocks(stacked).reshape(members, 2, 2, row_count, channels)
    return local_forward(spread[:, 0], spread[:, 1])


def fourier_inverse(real_part, imag_part):
    members, pairs, row_count, channels = real_part.shape
    devices = lax.axis_size("outer") * lax.axis_size("inner")
    tile_rows = row_count // devices
    length = 2 * row_count * devices
    real_part, imag_part = local_inverse(real_part, imag_part)
    parity = jnp.arange(2, dtype=jnp.int32)
    frequency = 2 * self_position() + parity
    twiddle = unit_angles(
        frequency[:, None] * jnp.arange(row_count, dtype=jnp.int32)[None, :], length
    )[:, :, None]
    real_part, imag_part = turned(real_part, imag_part, jnp.cos(twiddle), jnp.sin(twiddle), 1.0)
    stacked = jnp.stack([real_part, imag_part], axis=1).reshape(
        members * 4, devices, tile_rows * channels
    )
    gathered = spectral_blocks(stacked).reshape(members, 2, 2, devices, tile_rows * channels)
    target = jnp.arange(devices, dtype=jnp.int32)
    angles = unit_angles(
        target[:, None, None] * (2 * target[None, None, :] + parity[None, :, None]), 2 * devices
    )
    cosine = jnp.cos(angles)
    sine = jnp.sin(angles)
    scale = 1.0 / length
    real_out = (
        jnp.einsum("btd,mtdx->mbx", cosine, gathered[:, 0], precision=exact_mode)
        - jnp.einsum("btd,mtdx->mbx", sine, gathered[:, 1], precision=exact_mode)
    ) * scale
    imag_out = real_out[:0]
    return (real_out, imag_out)


def on_device(
    query_stream, key_stream, value_stream, filter_taps, skip_gain, short_weights, cotangent
):
    row_count, channels = query_stream.shape
    devices = lax.axis_size("outer") * lax.axis_size("inner")
    streams = jnp.stack([query_stream, key_stream, value_stream])
    earlier = passed_along(streams[:, row_count - 2 :, :], ("outer", "inner"), 1)
    ahead = jnp.concatenate([earlier, streams], axis=1)
    lag_one = ahead[:, 1 : row_count + 1]
    lag_two = ahead[:, 0:row_count]
    mixed = (
        short_weights[:, 0:1] * streams
        + short_weights[:, 1:2] * lag_one
        + short_weights[:, 2:3] * lag_two
    )
    product = mixed[1] * mixed[2]
    upstream = cotangent * mixed[0]
    spec_real, spec_imag = fourier_forward(jnp.stack([filter_taps, product, upstream]))
    filter_real, product_real, upstream_real = (spec_real[0], spec_real[1], spec_real[2])
    filter_imag, product_imag, upstream_imag = (spec_imag[0], spec_imag[1], spec_imag[2])
    causal_real = filter_real * product_real - filter_imag * product_imag
    causal_imag = filter_real * product_imag + filter_imag * product_real
    back_real = filter_real * upstream_real + filter_imag * upstream_imag
    back_imag = filter_real * upstream_imag - filter_imag * upstream_real
    grad_real = product_real * upstream_real + product_imag * upstream_imag
    grad_imag = product_real * upstream_imag - product_imag * upstream_real
    real_out, imag_out = fourier_inverse(
        jnp.stack([causal_real, back_real, grad_real]),
        jnp.stack([causal_imag, back_imag, grad_imag]),
    )
    longs = sequence_blocks(real_out).reshape(3, row_count, channels)
    summed = longs[0] + skip_gain * product
    gated_output = mixed[0] * summed
    backward = longs[1] + skip_gain * upstream
    grads = jnp.stack([cotangent * summed, backward * mixed[2], backward * mixed[1]])
    later = passed_along(grads[:, 0:2, :], ("outer", "inner"), -1)
    behind = jnp.concatenate([grads, later], axis=1)
    stream_grads = (
        short_weights[:, 0:1] * grads
        + short_weights[:, 1:2] * behind[:, 1 : row_count + 1]
        + short_weights[:, 2:3] * behind[:, 2 : row_count + 2]
    )
    tap_terms = jnp.stack(
        [
            jnp.sum(grads * streams, axis=1),
            jnp.sum(grads * lag_one, axis=1),
            jnp.sum(grads * lag_two, axis=1),
        ],
        axis=1,
    )
    skip_terms = jnp.sum(upstream * product, axis=0)
    tap_total, skip_total = lax.psum((tap_terms, skip_terms), ("outer", "inner"))
    factor = 1.0 / math.sqrt(row_count * devices)
    return (gated_output, stream_grads, longs[2] * factor, tap_total * factor, skip_total * factor)


LANES = 128


def halves(table):
    high = table.astype(ml_dtypes.bfloat16)
    low = (table - high.astype(np.float64)).astype(ml_dtypes.bfloat16)
    return high, low


def fourier_tables(devices, pieces):
    outer_size = devices * pieces
    length = outer_size * LANES
    place = np.arange(outer_size)
    place = (place % devices) * pieces + place // devices
    low = np.arange(outer_size)
    lane = np.arange(LANES)
    angle = 2.0 * np.pi / (4 * outer_size) * ((4 * low[:, None] + 1) * place[None, :] % (4 * outer_size))
    rows = np.concatenate([np.cos(angle), -np.sin(angle)], axis=0)
    row_high, row_low = halves(rows)
    forward_rows = np.concatenate([row_high, row_low, row_high], axis=1)
    back_high, back_low = halves(rows.T / length)
    inverse_rows = np.concatenate([back_high, back_low, back_high], axis=1)
    turn = 2.0 * np.pi / (4 * length) * ((4 * low[:, None] + 1) * lane[None, :] % (4 * length))
    twiddle = np.stack([np.cos(turn), -np.sin(turn)]).astype(np.float32)
    angle = 2.0 * np.pi / LANES * (lane[:, None] * lane[None, :] % LANES)
    cosine, sine = np.cos(angle), -np.sin(angle)
    forward = np.block([[cosine, sine], [-sine, cosine]])
    inverse = np.block([[cosine, -sine], [sine, cosine]])
    columns = np.stack([*halves(forward), *halves(inverse)])
    return forward_rows, inverse_rows, columns, twiddle


def split(value):
    high = value.astype(jnp.bfloat16)
    return high, (value - high.astype(jnp.float32)).astype(jnp.bfloat16)


def dot(left, right):
    return jnp.dot(left, right, preferred_element_type=jnp.float32)


def three_dots(value, high_table, low_table):
    high, low = split(value)
    return dot(high, high_table) + dot(high, low_table) + dot(low, high_table)


def kernel(
    outer_count,
    inner_count,
    query_hbm,
    key_hbm,
    value_hbm,
    taps_hbm,
    gain_hbm,
    weights_hbm,
    cotangent_hbm,
    forward_hbm,
    inverse_hbm,
    columns_hbm,
    twiddle_hbm,
    gated_ref,
    stream_grads_ref,
    filter_grad_ref,
    tap_grads_ref,
    skip_grad_ref,
    streams,
    mixed,
    product,
    upstream,
    grads,
    sent,
    arrived,
    spectra,
    sent_back,
    arrived_back,
    sums,
    sums_in,
    totals,
    totals_in,
    send_sems,
    recv_sems,
    halo_send,
    halo_recv,
    sum_send,
    sum_recv,
    taps_ref,
    gain_ref,
    weights_ref,
    cotangent_ref,
    forward_ref,
    inverse_ref,
    columns_ref,
    twiddle_ref,
    load_sems,
):
    devices = outer_count * inner_count
    row_count = query_hbm.shape[0]
    pieces = row_count // LANES
    owned = LANES // devices
    tile = owned * pieces
    outer_size = devices * pieces
    my_outer = lax.axis_index("outer")
    my_inner = lax.axis_index("inner")
    me = my_outer * inner_count + my_inner

    def device(index):
        return (index // inner_count, index % inner_count)

    barrier = pltpu.get_barrier_semaphore()

    def greet(step, carry):
        pl.semaphore_signal(
            barrier, inc=1, device_id=device((me + step) % devices), device_id_type=MESH
        )
        return carry

    lax.fori_loop(1, devices, greet, 0)

    stream_hbms = (query_hbm, key_hbm, value_hbm)
    loads = {}
    for at, (name, source, target) in enumerate(
        [
            ("taps", taps_hbm, taps_ref),
            ("key", key_hbm, streams.at[1, pl.ds(8, row_count), :]),
            ("value", value_hbm, streams.at[2, pl.ds(8, row_count), :]),
            ("query", query_hbm, streams.at[0, pl.ds(8, row_count), :]),
            ("weights", weights_hbm, weights_ref),
            ("cotangent", cotangent_hbm, cotangent_ref),
            ("forward", forward_hbm, forward_ref),
            ("twiddle", twiddle_hbm, twiddle_ref),
            ("columns", columns_hbm, columns_ref),
            ("inverse", inverse_hbm, inverse_ref),
            ("gain", gain_hbm, gain_ref),
        ]
    ):
        loads[name] = pltpu.make_async_copy(source, target, load_sems.at[at])
        loads[name].start()

    following = (me + 1) % devices
    preceding = (me + devices - 1) % devices
    halo_copies = [
        pltpu.make_async_remote_copy(
            src_ref=stream_hbms[s].at[pl.ds(row_count - 8, 8), :],
            dst_ref=streams.at[s, pl.ds(0, 8), :],
            send_sem=halo_send.at[s],
            recv_sem=halo_recv.at[s],
            device_id=device(following),
            device_id_type=MESH,
        )
        for s in range(3)
    ]

    group = 4 if inner_count % 4 == 0 else inner_count
    places = inner_count // group
    planes = outer_count * group
    my_place = my_inner // group
    my_member = my_outer * group + my_inner % group

    near_places = [lax.rem(my_place + places - shift, places) for shift in range(places)]

    def mine():
        return pl.ds(pl.multiple_of(me * tile, tile), tile)

    def exchange(source, target, group_at, signal):
        def send(outer, member, shift):
            inner = near_places[shift] * group + member
            start = pl.multiple_of((outer * inner_count + inner) * tile, tile)
            pltpu.make_async_remote_copy(
                src_ref=source.at[signal, pl.ds(start, tile), :],
                dst_ref=target.at[signal, mine(), :],
                send_sem=send_sems.at[group_at, signal],
                recv_sem=recv_sems.at[group_at, signal],
                device_id=(outer, inner),
                device_id_type=MESH,
            ).start()

        def send_places(turn, carry):
            outer = lax.rem(my_outer + turn, outer_count)
            member = lax.rem(my_inner + lax.div(turn, outer_count), group)
            for shift in (*range(places // 2, places), *range(places // 2)):
                send(outer, member, shift)
            return carry

        lax.fori_loop(1, planes, send_places, 0)
        for shift in range(1, places):
            send(my_outer, lax.rem(my_inner, group), shift)
        target[signal, mine(), :] = source[signal, mine(), :]

    def all_but_one(buffer, signal):
        return buffer.at[signal, pl.ds(0, (devices - 1) * tile), :]

    def received(target, group, signal):
        view = all_but_one(target, signal)
        pltpu.make_async_copy(view, view, recv_sems.at[group, signal]).wait()

    def drained(source, group, signal):
        view = all_but_one(source, signal)
        pltpu.make_async_copy(view, view, send_sems.at[group, signal]).wait()

    def put(block, signal, piece):
        sent[signal, pl.ds(piece, LANES, stride=pieces), :] = block.T

    loads["taps"].wait()
    for piece in range(pieces):
        put(taps_ref[pl.ds(piece * LANES, LANES), :], 0, piece)
    pl.semaphore_wait(barrier, devices - 1)

    for copy in halo_copies:
        copy.start()
    exchange(sent, arrived, 0, 0)

    for name in ("key", "value", "query", "weights", "cotangent"):
        loads[name].wait()
    for copy in halo_copies:
        copy.wait()
    for s in range(3):
        streams[s, pl.ds(0, 8), :] = jnp.where(me > 0, streams[s, pl.ds(0, 8), :], 0.0)

    def mix(s, piece):
        base = 8 + piece * LANES
        return (
            weights_ref[s, 0:1, :] * streams[s, pl.ds(base, LANES), :]
            + weights_ref[s, 1:2, :] * streams[s, pl.ds(base - 1, LANES), :]
            + weights_ref[s, 2:3, :] * streams[s, pl.ds(base - 2, LANES), :]
        )

    for piece in range(pieces):
        rows = pl.ds(piece * LANES, LANES)
        key, value = mix(1, piece), mix(2, piece)
        mixed[1, rows, :] = key
        mixed[2, rows, :] = value
        product[rows, :] = key * value
        put(key * value, 1, piece)
    exchange(sent, arrived, 0, 1)
    skip_sum = jnp.zeros((1, LANES), jnp.float32)
    for piece in range(pieces):
        rows = pl.ds(piece * LANES, LANES)
        query = mix(0, piece)
        mixed[0, rows, :] = query
        rising = cotangent_ref[rows, :] * query
        upstream[rows, :] = rising
        put(rising, 2, piece)
        skip_sum += jnp.sum(rising * product[rows, :], axis=0, keepdims=True)
    exchange(sent, arrived, 0, 2)

    for name in ("forward", "twiddle", "columns", "inverse", "gain"):
        loads[name].wait()
    twiddle_real = twiddle_ref[0]
    twiddle_imag = twiddle_ref[1]

    def transform(signal):
        received(arrived, 0, signal)
        for c in range(owned):
            block = jnp.concatenate(
                [
                    arrived[signal, pl.ds(c * pieces + piece, devices, stride=tile), :]
                    for piece in range(pieces)
                ],
                axis=0,
            )
            high, low = split(block)
            first = dot(forward_ref[...], jnp.concatenate([high, high, low], axis=0))
            real, imag = first[:outer_size], first[outer_size:]
            turned_block = jnp.concatenate(
                [
                    real * twiddle_real - imag * twiddle_imag,
                    real * twiddle_imag + imag * twiddle_real,
                ],
                axis=1,
            )
            spectra[signal, c] = three_dots(turned_block, columns_ref[0], columns_ref[1])

    def back(first, second, conjugated, signal):
        for c in range(owned):
            one, two = spectra[first, c], spectra[second, c]
            one_real, one_imag = one[:, :LANES], one[:, LANES:]
            two_real, two_imag = two[:, :LANES], two[:, LANES:]
            if conjugated:
                real = one_real * two_real + one_imag * two_imag
                imag = one_real * two_imag - one_imag * two_real
            else:
                real = one_real * two_real - one_imag * two_imag
                imag = one_real * two_imag + one_imag * two_real
            inner = three_dots(
                jnp.concatenate([real, imag], axis=1), columns_ref[2], columns_ref[3]
            )
            real, imag = inner[:, :LANES], inner[:, LANES:]
            turned_block = jnp.concatenate(
                [
                    real * twiddle_real + imag * twiddle_imag,
                    imag * twiddle_real - real * twiddle_imag,
                ],
                axis=0,
            )
            high, low = split(turned_block)
            block = dot(inverse_ref[...], jnp.concatenate([high, high, low], axis=0))
            for piece in range(pieces):
                sent_back[signal, pl.ds(c * pieces + piece, devices, stride=tile), :] = block[
                    piece * devices : (piece + 1) * devices
                ]
        exchange(sent_back, arrived_back, 1, signal)

    transform(0)
    transform(1)
    back(0, 1, False, 0)
    transform(2)
    back(0, 2, True, 1)
    back(1, 2, True, 2)

    def piece_of(signal, piece):
        return arrived_back[signal, pl.ds(piece, LANES, stride=pieces), :].T

    gain = gain_ref[...]
    tap_sums = [[jnp.zeros((1, LANES), jnp.float32) for _ in range(3)] for _ in range(3)]

    def add_taps(s, piece, values):
        for j in range(3):
            earlier = streams[s, pl.ds(8 + piece * LANES - j, LANES), :]
            tap_sums[s][j] += jnp.sum(values * earlier, axis=0, keepdims=True)

    received(arrived_back, 1, 0)
    for piece in range(pieces):
        rows = pl.ds(piece * LANES, LANES)
        summed = piece_of(0, piece) + gain * product[rows, :]
        gated_ref[rows, :] = mixed[0, rows, :] * summed
        values = cotangent_ref[rows, :] * summed
        grads[0, rows, :] = values
        add_taps(0, piece, values)
    received(arrived_back, 1, 1)
    for piece in range(pieces):
        rows = pl.ds(piece * LANES, LANES)
        backward = piece_of(1, piece) + gain * upstream[rows, :]
        for s in (1, 2):
            values = backward * mixed[3 - s, rows, :]
            grads[s, rows, :] = values
            add_taps(s, piece, values)

    grad_halo = pltpu.make_async_remote_copy(
        src_ref=grads.at[:, pl.ds(0, 8), :],
        dst_ref=grads.at[:, pl.ds(row_count, 8), :],
        send_sem=halo_send.at[3],
        recv_sem=halo_recv.at[3],
        device_id=device(preceding),
        device_id_type=MESH,
    )
    grad_halo.start()

    listed = [tap_sums[s][j] for s in range(3) for j in range(3)] + [skip_sum]
    for at, row in enumerate(listed):
        sums[at : at + 1, :] = row
    sums[10:16, :] = jnp.zeros((6, LANES), jnp.float32)
    sums_in[my_member] = sums[...]

    def send_sums(step, carry):
        member = (my_member + step) % planes
        pltpu.make_async_remote_copy(
            src_ref=sums,
            dst_ref=sums_in.at[my_member],
            send_sem=sum_send.at[0],
            recv_sem=sum_recv.at[0],
            device_id=(member // group, my_place * group + member % group),
            device_id_type=MESH,
        ).start()
        return carry

    lax.fori_loop(1, planes, send_sums, 0)

    def stream_grad(s, start, size):
        return (
            weights_ref[s, 0:1, :] * grads[s, pl.ds(start, size), :]
            + weights_ref[s, 1:2, :] * grads[s, pl.ds(start + 1, size), :]
            + weights_ref[s, 2:3, :] * grads[s, pl.ds(start + 2, size), :]
        )

    for s in range(3):
        for start in range(0, row_count, LANES):
            size = min(LANES, row_count - 8 - start)
            stream_grads_ref[s, pl.ds(start, size), :] = stream_grad(s, start, size)

    def take(view, semaphore):
        pltpu.make_async_copy(view, view, semaphore).wait()

    take(sums_in.at[pl.ds(0, planes - 1)], sum_recv.at[0])
    total = sums_in[0]
    for member in range(1, planes):
        total += sums_in[member]
    totals[...] = total
    totals_in[my_place] = total

    def send_totals(step, carry):
        place = (my_place + step) % places
        pltpu.make_async_remote_copy(
            src_ref=totals,
            dst_ref=totals_in.at[my_place],
            send_sem=sum_send.at[1],
            recv_sem=sum_recv.at[1],
            device_id=(my_outer, place * group + my_inner % group),
            device_id_type=MESH,
        ).start()
        return carry

    lax.fori_loop(1, places, send_totals, 0)

    grad_halo.wait()
    grads[:, pl.ds(row_count, 8), :] = jnp.where(
        me < devices - 1, grads[:, pl.ds(row_count, 8), :], 0.0
    )
    for s in range(3):
        stream_grads_ref[s, pl.ds(row_count - 8, 8), :] = stream_grad(s, row_count - 8, 8)

    factor = 1.0 / math.sqrt(row_count * devices)
    received(arrived_back, 1, 2)
    for piece in range(pieces):
        filter_grad_ref[pl.ds(piece * LANES, LANES), :] = piece_of(2, piece) * factor

    if places > 1:
        take(totals_in.at[pl.ds(0, places - 1)], sum_recv.at[1])
    total = totals_in[0]
    for place in range(1, places):
        total += totals_in[place]
    total = total * factor
    for s in range(3):
        tap_grads_ref[s] = total[3 * s : 3 * s + 3, :]
    skip_grad_ref[...] = total[9:10, :]

    for signal in range(3):
        drained(sent, 0, signal)
        drained(sent_back, 1, signal)
    take(sums_in.at[pl.ds(0, planes - 1)], sum_send.at[0])
    if places > 1:
        take(totals_in.at[pl.ds(0, places - 1)], sum_send.at[1])


def store_kernel(*refs):
    sources, targets, sems = refs[:5], refs[5:10], refs[10]
    copies = [
        pltpu.make_async_copy(source, target, sems.at[at])
        for at, (source, target) in enumerate(zip(sources, targets))
    ]
    for copy in copies:
        copy.start()
    for copy in copies:
        copy.wait()


def by_channel(
    outer_count,
    inner_count,
    query_stream,
    key_stream,
    value_stream,
    filter_taps,
    skip_gain,
    short_weights,
    cotangent,
):
    row_count, channels = query_stream.shape
    devices = outer_count * inner_count
    pieces = row_count // LANES
    owned = channels // devices
    tables = fourier_tables(devices, pieces)
    group = 4 if inner_count % 4 == 0 else inner_count
    whole = pltpu.VMEM((row_count, channels), jnp.float32)
    three = pltpu.VMEM((3, row_count, channels), jnp.float32)
    padded = pltpu.VMEM((3, row_count + 8, channels), jnp.float32)
    vmem = pl.BlockSpec(memory_space=pltpu.VMEM)
    outs = pl.pallas_call(
        functools.partial(kernel, outer_count, inner_count),
        out_shape=(
            jax.ShapeDtypeStruct((row_count, channels), jnp.float32),
            jax.ShapeDtypeStruct((3, row_count, channels), jnp.float32),
            jax.ShapeDtypeStruct((row_count, channels), jnp.float32),
            jax.ShapeDtypeStruct((3, 3, channels), jnp.float32),
            jax.ShapeDtypeStruct((1, channels), jnp.float32),
        ),
        in_specs=[pl.BlockSpec(memory_space=pltpu.HBM)] * 11,
        out_specs=(vmem,) * 5,
        scratch_shapes=[
            padded,
            three,
            whole,
            whole,
            padded,
            three,
            three,
            pltpu.VMEM((3, owned, devices * pieces, 2 * LANES), jnp.float32),
            three,
            three,
            pltpu.VMEM((16, channels), jnp.float32),
            pltpu.VMEM((outer_count * group, 16, channels), jnp.float32),
            pltpu.VMEM((16, channels), jnp.float32),
            pltpu.VMEM((inner_count // group, 16, channels), jnp.float32),
            pltpu.SemaphoreType.DMA((2, 3)),
            pltpu.SemaphoreType.DMA((2, 3)),
            pltpu.SemaphoreType.DMA((4,)),
            pltpu.SemaphoreType.DMA((4,)),
            pltpu.SemaphoreType.DMA((2,)),
            pltpu.SemaphoreType.DMA((2,)),
            whole,
            pltpu.VMEM((1, channels), jnp.float32),
            pltpu.VMEM(short_weights.shape, jnp.float32),
            whole,
            *(pltpu.VMEM(table.shape, table.dtype) for table in tables),
            pltpu.SemaphoreType.DMA((11,)),
        ],
        compiler_params=pltpu.CompilerParams(
            collective_id=0, has_side_effects=True, vmem_limit_bytes=63 * 1024 * 1024
        ),
    )(
        query_stream,
        key_stream,
        value_stream,
        filter_taps,
        skip_gain.reshape(1, channels),
        short_weights,
        cotangent,
        *(jnp.asarray(table) for table in tables),
    )
    outs = pl.pallas_call(
        store_kernel,
        out_shape=tuple(jax.ShapeDtypeStruct(out.shape, out.dtype) for out in outs),
        in_specs=[vmem] * 5,
        out_specs=(pl.BlockSpec(memory_space=pltpu.HBM),) * 5,
        scratch_shapes=[pltpu.SemaphoreType.DMA((5,))],
    )(*outs)
    return (*outs[:4], outs[4].reshape(channels))


def either_plan(outer_count, inner_count, query_stream, *others):
    row_count, channels = query_stream.shape
    devices = outer_count * inner_count
    even = (
        channels == LANES
        and row_count % LANES == 0
        and channels % devices == 0
        and (channels // devices) * (row_count // LANES) % 8 == 0
        and devices % 8 == 0
    )
    if even:
        return by_channel(outer_count, inner_count, query_stream, *others)
    return on_device(query_stream, *others)


def solution(mesh):
    placed = (
        P(("outer", "inner"), None),
        P(("outer", "inner"), None),
        P(("outer", "inner"), None),
        P(("outer", "inner"), None),
        P(),
        P(),
        P(("outer", "inner"), None),
    )
    return jax.shard_map(
        functools.partial(either_plan, mesh.shape["outer"], mesh.shape["inner"]),
        mesh=mesh,
        in_specs=placed,
        out_specs=(
            P(("outer", "inner"), None),
            P(None, ("outer", "inner"), None),
            P(("outer", "inner"), None),
            P(),
            P(),
        ),
        check_vma=False,
    )
```
